32 devices in a mesh: fsdp: 16 (over z, y, x), tp: 2 (over core).
Axes of the slice: x: 2, y: 2, z: 4, core: 2. Of those that a mesh axis runs over, the one named last changes fastest.
Arguments:
- hidden_in: bfloat16 [16384, 1024], P(('fsdp', 'tp')), may hold values from -6 to 6
- out_grad: bfloat16 [16384, 1024], P(('fsdp', 'tp')), may hold values from -6 to 6
- seq_lengths: int32 [16, 4], P('fsdp'), may hold values from 1 to 768, 1024 in all within a row
- norm_gain: float32 [1024], replicated, may hold values from 0.5 to 1.5
- w_z: bfloat16 [1024, 1536], P('fsdp', 'tp'), may hold values from -0.1875 to 0.1875
- w_x: bfloat16 [1024, 1536], P('fsdp', 'tp'), may hold values from -0.1875 to 0.1875
- w_bc: bfloat16 [1024, 256], P('fsdp'), may hold values from -0.1875 to 0.1875
- w_dt: bfloat16 [1024, 24], P('fsdp', 'tp'), may hold values from -0.1875 to 0.1875
- conv_x: float32 [4, 1536], replicated, may hold values from -3 to 3
- conv_bc: float32 [4, 256], replicated, may hold values from -3 to 3
- dt_bias: float32 [24], replicated, may hold values from -9 to -2
- a_log: float32 [24], replicated, may hold values from 0 to 2.5
- d_skip: float32 [24], replicated, may hold values from 0.5 to 2
- w_q: bfloat16 [1024, 512], P('fsdp', 'tp'), may hold values from -0.1875 to 0.1875
- key_matrix: bfloat16 [1024, 128], P('fsdp', 'tp'), may hold values from -0.1875 to 0.1875
- value_matrix: bfloat16 [1024, 128], P('fsdp', 'tp'), may hold values from -0.1875 to 0.1875
- w_o: bfloat16 [512, 1024], P('tp', 'fsdp'), may hold values from -1.5 to 1.5
- w_out: bfloat16 [1536, 1024], P('tp', 'fsdp'), may hold values from -0.15625 to 0.15625
- ff_gain: float32 [1024], replicated, may hold values from 0.5 to 1.5
- w_gate: bfloat16 [1024, 2048], P('fsdp', 'tp'), may hold values from -0.1875 to 0.1875
- w_up: bfloat16 [1024, 2048], P('fsdp', 'tp'), may hold values from -0.1875 to 0.1875
- w_down: bfloat16 [2048, 1024], P('tp', 'fsdp'), may hold values from -0.125 to 0.125
Outputs:
- layer_out: bfloat16 [16384, 1024], P(('fsdp', 'tp'))
- input_grad: bfloat16 [16384, 1024], P(('fsdp', 'tp'))
- norm_gain_grad: float32 [1024], replicated
- w_z_grad: float32 [1024, 1536], P('fsdp', 'tp')
- w_x_grad: float32 [1024, 1536], P('fsdp', 'tp')
- w_bc_grad: float32 [1024, 256], P('fsdp')
- w_dt_grad: float32 [1024, 24], P('fsdp', 'tp')
- conv_x_grad: float32 [4, 1536], replicated
- conv_bc_grad: float32 [4, 256], replicated
- dt_bias_grad: float32 [24], replicated
- a_log_grad: float32 [24], replicated
- d_skip_grad: float32 [24], replicated
- w_q_grad: float32 [1024, 512], P('fsdp', 'tp')
- w_k_grad: float32 [1024, 128], P('fsdp', 'tp')
- w_v_grad: float32 [1024, 128], P('fsdp', 'tp')
- w_o_grad: float32 [512, 1024], P('tp', 'fsdp')
- w_out_grad: float32 [1536, 1024], P('tp', 'fsdp')
- ff_gain_grad: float32 [1024], replicated
- w_gate_grad: float32 [1024, 2048], P('fsdp', 'tp')
- w_up_grad: float32 [1024, 2048], P('fsdp', 'tp')
- w_down_grad: float32 [2048, 1024], P('tp', 'fsdp')
The draws below stay inside these ranges and needn't reach their ends.
Inputs may be any that keep to these rules, and one draw needn't show every extreme that they name: `seq_lengths`: row f holds the 4 document lengths of data shard f in order; they sum to 1024, and the longest of each row is exactly 768.
All inputs are finite; a program needn't handle non-finite values.
Results may differ from the reference program's by a relative error of at most 0.015.
Values may be sent and summed in bfloat16 or wider, within the bound.
A program may use at most 192 MiB of HBM per device.

```python
import math
import jax
import jax.numpy as jnp
import numpy as np
from jax import lax

MODEL_WIDTH = 1024
FF = 2048
HQ = 8
KEY_VALUE_HEADS = 2
HEAD_WIDTH = 64
MH = 24
NS = 128
KC = 4
DS = 1536
ROWS = 1024
DOCS = 4
SEQ_MOST = 768
SPAN = 256
ATT_BLOCK = 512
TOKENS = 16384
N_FSDP = 16


def block_scale(stream_key, extent, pieces, least, largest):
    def one(dim, blocks):
        heights = jax.random.uniform(jax.random.fold_in(jax.random.fold_in(stream_key, 6), dim), (blocks,), jnp.float32, least / len(pieces), largest / len(pieces))
        return jnp.repeat(jnp.exp(heights), extent[dim] // blocks).reshape((-1,) + (1,) * (len(extent) - dim - 1))

    loudness = one(*pieces[0])
    for cut in pieces[1:]:
        loudness = loudness * one(*cut)
    return loudness


def split_up(number_of, total, reach, lean):
    weights = [(1 << 20) // math.isqrt(grade ** lean) + 1 for grade in range(2, number_of + 1)]
    rest, holding = total - reach - (number_of - 1), [1] * (number_of - 1)
    while rest > 0:
        movable = [i for i in range(number_of - 1) if holding[i] < reach]
        pool, remaining = sum([weights[i] for i in movable]), rest
        for i in movable:
            extra = min(reach - holding[i], max(1, remaining * weights[i] // pool), rest)
            holding[i] = holding[i] + extra
            rest = rest - extra
    return np.array([reach] + holding)


def uneven(key, amount, total, most, skew):
    if amount == 2:
        one = jax.random.randint(key, (), max(1, total - most), min(most, total - 1) + 1)
        return jnp.stack([one, total - one])
    sizes = jnp.asarray(split_up(amount, total, most, skew), jnp.int32)
    pairs = (amount - 1) // 2
    donor, taker = sizes[1:1 + 2 * pairs:2], sizes[2:2 + 2 * pairs:2]
    margin = jnp.minimum(donor - 1, most - taker)
    passed = jax.random.randint(jax.random.fold_in(key, 1), (pairs,), 0, 1 << 20) % (margin + 1)
    sizes = sizes.at[1:1 + 2 * pairs:2].set(donor - passed).at[2:2 + 2 * pairs:2].set(taker + passed)
    return sizes[jax.random.permutation(jax.random.fold_in(key, 2), amount)]


def gaussian(own_key, extent, scale, bound, shards=(), held_as=jnp.bfloat16):
    loudness = block_scale(own_key, extent, shards, -0.22, 0.18) if shards else 1.0
    array = jax.random.normal(own_key, extent, jnp.float32) * scale * loudness
    return jnp.minimum(jnp.maximum(array, -bound), bound).astype(held_as)


def setup_inputs(seed: int = 0) -> dict:
    seeds = jax.random.split(jax.random.key(seed), 23)
    return {
        "hidden_in": gaussian(seeds[0], (TOKENS, MODEL_WIDTH), 1.0, 6.0, ((0, 32),)),
        "out_grad": gaussian(seeds[1], (TOKENS, MODEL_WIDTH), 1.0, 6.0, ((0, 32),)),
        "seq_lengths": jax.vmap(lambda own: uneven(own, DOCS, ROWS, SEQ_MOST, 2))(jax.random.split(seeds[2], N_FSDP)).reshape((N_FSDP, DOCS)).astype(jnp.int32),
        "norm_gain": jnp.clip(1.0 + 0.1 * jax.random.normal(seeds[3], (MODEL_WIDTH,), jnp.float32), 0.5, 1.5),
        "w_z": gaussian(seeds[4], (MODEL_WIDTH, DS), MODEL_WIDTH ** -0.5, 0.1875, ((0, 16), (1, 2))),
        "w_x": gaussian(seeds[5], (MODEL_WIDTH, DS), MODEL_WIDTH ** -0.5, 0.1875, ((0, 16), (1, 2))),
        "w_bc": gaussian(seeds[6], (MODEL_WIDTH, 2 * NS), MODEL_WIDTH ** -0.5, 0.1875, ((0, 16),)),
        "w_dt": gaussian(seeds[7], (MODEL_WIDTH, MH), MODEL_WIDTH ** -0.5, 0.1875, ((0, 16), (1, 2))),
        "conv_x": gaussian(seeds[8], (KC, DS), KC ** -0.5, 3.0, (), jnp.float32),
        "conv_bc": gaussian(seeds[9], (KC, 2 * NS), KC ** -0.5, 3.0, (), jnp.float32),
        "dt_bias": jnp.clip(jax.random.uniform(seeds[10], (MH,), jnp.float32, -9.0, -2.0), -9.0, -2.0),
        "a_log": jnp.clip(jax.random.uniform(seeds[11], (MH,), jnp.float32, 0.0, 2.5), 0.0, 2.5),
        "d_skip": jnp.clip(jax.random.uniform(seeds[12], (MH,), jnp.float32, 0.5, 2.0), 0.5, 2.0),
        "w_q": gaussian(seeds[13], (MODEL_WIDTH, HQ * HEAD_WIDTH), MODEL_WIDTH ** -0.5, 0.1875, ((0, 16), (1, 2))),
        "key_matrix": gaussian(seeds[14], (MODEL_WIDTH, KEY_VALUE_HEADS * HEAD_WIDTH), MODEL_WIDTH ** -0.5, 0.1875, ((0, 16), (1, 2))),
        "value_matrix": gaussian(seeds[15], (MODEL_WIDTH, KEY_VALUE_HEADS * HEAD_WIDTH), MODEL_WIDTH ** -0.5, 0.1875, ((0, 16), (1, 2))),
        "w_o": gaussian(seeds[16], (HQ * HEAD_WIDTH, MODEL_WIDTH), (HQ * HEAD_WIDTH // 32) ** -0.5, 1.5, ((0, 2), (1, 16))),
        "w_out": gaussian(seeds[17], (DS, MODEL_WIDTH), DS ** -0.5, 0.15625, ((0, 2), (1, 16))),
        "ff_gain": jnp.clip(1.0 + 0.1 * jax.random.normal(seeds[18], (MODEL_WIDTH,), jnp.float32), 0.5, 1.5),
        "w_gate": gaussian(seeds[19], (MODEL_WIDTH, FF), MODEL_WIDTH ** -0.5, 0.1875, ((0, 16), (1, 2))),
        "w_up": gaussian(seeds[20], (MODEL_WIDTH, FF), MODEL_WIDTH ** -0.5, 0.1875, ((0, 16), (1, 2))),
        "w_down": gaussian(seeds[21], (FF, MODEL_WIDTH), FF ** -0.5, 0.125, ((0, 2), (1, 16))),
    }


EPSILON = 1e-05
ROPE_BASE = 10000.0
HIGH = lax.Precision.HIGHEST
MASKED = -1e+30

@jax.custom_vjp
def low(v):
    return lax.optimization_barrier(v.astype(jnp.bfloat16)).astype(jnp.float32)

@jax.custom_vjp
def low_back(v):
    return v

def low_keep(v):
    return (low(v), None)

def low_pass(kept, grad):
    return (grad,)

def back_keep(v):
    return (v, None)

def back_low(kept, grad):
    return (low(grad),)
low.defvjp(low_keep, low_pass)
low_back.defvjp(back_keep, back_low)

def product_high(left, right):
    return jnp.dot(left, right, precision=HIGH, preferred_element_type=jnp.float32)

def doc_tables(lengths, row_count):
    lengths = lengths.astype(jnp.int32)
    ends = jnp.cumsum(lengths).astype(jnp.int32)
    index = jnp.arange(row_count, dtype=jnp.int32)
    segment = lax.optimization_barrier(jnp.sum((index[:, None] >= ends[None, :]).astype(jnp.int32), axis=1)).astype(jnp.int32)
    starts = (ends - lengths).astype(jnp.int32)
    member = segment[:, None] == jnp.arange(lengths.shape[0], dtype=jnp.int32)[None, :]
    begin = lax.optimization_barrier(jnp.sum(jnp.where(member, starts[None, :], 0), axis=1)).astype(jnp.int32)
    return (segment, (index - begin).astype(jnp.int32))

def rms_scale(values, gain):
    factor = lax.rsqrt(lax.optimization_barrier(jnp.mean(values * values, axis=-1, keepdims=True)) + EPSILON)
    return values * factor * gain

def causal_conv(values, taps, segment):
    width = taps.shape[0]
    total = values * taps[width - 1]
    for delay in range(1, width):
        earlier = jnp.concatenate([jnp.zeros((delay, values.shape[1]), values.dtype), values[:-delay]], axis=0)
        joined = jnp.concatenate([jnp.zeros((delay,), values.dtype), (segment[delay:] == segment[:-delay]).astype(values.dtype)])
        total = total + earlier * joined[:, None] * taps[width - 1 - delay]
    return total

def rotate(values, position):
    row_count = values.shape[0]
    shaped = values.reshape(row_count, -1, HEAD_WIDTH)
    halfway = HEAD_WIDTH // 2
    frequency = ROPE_BASE ** (-2.0 * jnp.arange(halfway, dtype=jnp.float32) / HEAD_WIDTH)
    angle = position.astype(jnp.float32)[:, None, None] * frequency[None, None, :]
    cosine = jnp.cos(angle)
    sine = jnp.sin(angle)
    first = shaped[..., :halfway]
    second = shaped[..., halfway:]
    turned = jnp.concatenate([first * cosine - second * sine, second * cosine + first * sine], axis=-1)
    return turned.reshape(row_count, -1)

def span_scan(x_heads, b_vectors, c_vectors, step_size, rate, segment):
    row_count, heads, head_size = x_heads.shape
    count = row_count // SPAN
    inside = jnp.arange(SPAN, dtype=jnp.int32)
    lower = inside[:, None] >= inside[None, :]

    def advance(carry, item):
        state, previous = carry
        block_x, block_b, block_c, block_step, block_seg = item
        decay_factor = jnp.cumsum(block_step * rate[None, :], axis=0)
        allowed = lower & (block_seg[:, None] == block_seg[None, :])
        spread = jnp.where(allowed[:, :, None], decay_factor[:, None, :] - decay_factor[None, :, :], MASKED)
        inner = jnp.dot(block_c, block_b.T, precision=HIGH, preferred_element_type=jnp.float32)
        mixing = jnp.exp(spread) * inner[:, :, None] * block_step[None, :, :]
        output = jnp.einsum('tsh,shp->thp', mixing, block_x, precision=HIGH)
        carried = (block_seg == previous).astype(jnp.float32)[:, None] * jnp.exp(decay_factor)
        output = output + jnp.einsum('tn,hpn->thp', block_c, state, precision=HIGH) * carried[:, :, None]
        tail = (block_seg == block_seg[-1]).astype(jnp.float32)[:, None] * jnp.exp(decay_factor[-1][None, :] - decay_factor) * block_step
        state = state * carried[-1][:, None, None] + jnp.einsum('sh,shp,sn->hpn', tail, block_x, block_b, precision=HIGH)
        return ((state, block_seg[-1]), output)
    items = (x_heads.reshape(count, SPAN, heads, head_size), b_vectors.reshape(count, SPAN, -1), c_vectors.reshape(count, SPAN, -1), step_size.reshape(count, SPAN, heads), segment.reshape(count, SPAN))
    start = (jnp.zeros((heads, head_size, b_vectors.shape[1]), jnp.float32), jnp.asarray(-1, jnp.int32))
    _, outputs = lax.scan(jax.checkpoint(advance), start, items)
    return outputs.reshape(row_count, heads, head_size)

def mixer_middle(z_branch, x_branch, pair_branch, step_raw, conv_own, conv_pair, bias, log_rate, skip, segment):
    row_count = z_branch.shape[0]
    x_active = jax.nn.silu(causal_conv(x_branch, conv_own, segment))
    pair_active = jax.nn.silu(causal_conv(pair_branch, conv_pair, segment))
    step_size = jax.nn.softplus(step_raw + bias[None, :])
    rate = -jnp.exp(log_rate)
    heads = bias.shape[0]
    x_heads = x_active.reshape(row_count, heads, HEAD_WIDTH)
    states = span_scan(x_heads, pair_active[:, :NS], pair_active[:, NS:], step_size, rate, segment)
    result = states + skip[None, :, None] * x_heads
    return result.reshape(row_count, heads * HEAD_WIDTH) * jax.nn.silu(z_branch)

def attention(query, keys, values, segment):
    row_count = query.shape[0]
    kv_heads = keys.shape[1] // HEAD_WIDTH
    group = query.shape[1] // keys.shape[1]
    key_heads = keys.reshape(row_count, kv_heads, HEAD_WIDTH)
    value_heads = values.reshape(row_count, kv_heads, HEAD_WIDTH)
    index = jnp.arange(row_count, dtype=jnp.int32)
    count = row_count // ATT_BLOCK
    scale = 1.0 / math.sqrt(HEAD_WIDTH)

    def block(item):
        query_block, seg_block, row_block = item
        score = low_back(jnp.einsum('qkgd,skd->kgqs', query_block, key_heads, precision=HIGH) * scale)
        allowed = (seg_block[:, None] == segment[None, :]) & (row_block[:, None] >= index[None, :])
        score = jnp.where(allowed[None, None], score, MASKED)
        peak = lax.optimization_barrier(jnp.max(score, axis=-1, keepdims=True))
        weight = jnp.exp(score - peak)
        prob = low(weight / lax.optimization_barrier(jnp.sum(weight, axis=-1, keepdims=True)))
        output = jnp.einsum('kgqs,skd->qkgd', prob, value_heads, precision=HIGH)
        return output.reshape(ATT_BLOCK, kv_heads * group * HEAD_WIDTH)
    blocks = (query.reshape(count, ATT_BLOCK, kv_heads, group, HEAD_WIDTH), segment.reshape(count, ATT_BLOCK), index.reshape(count, ATT_BLOCK))
    return lax.map(jax.checkpoint(block), blocks).reshape(row_count, -1)

def layer(resident, segment, position, params):
    norm_gain, w_z, w_x, w_bc, w_dt, conv_x, conv_bc, dt_bias, a_log, d_skip, w_q, key_matrix, value_matrix, w_o, w_out, ff_gain, w_gate, w_up, w_down = params
    normed = low(rms_scale(resident, norm_gain))
    z_branch = low_back(product_high(normed, w_z))
    x_branch = low_back(product_high(normed, w_x))
    pair_branch = product_high(normed, w_bc)
    step_raw = low_back(product_high(normed, w_dt))
    gated = low(mixer_middle(z_branch, x_branch, pair_branch, step_raw, conv_x, conv_bc, dt_bias, a_log, d_skip, segment))
    query = low(rotate(low_back(product_high(normed, w_q)), position))
    keys = low(rotate(low_back(product_high(normed, key_matrix)), position))
    values = low(low_back(product_high(normed, value_matrix)))
    attended = low_back(low(attention(query, keys, values, segment)))
    branch = low_back(product_high(gated, w_out) + product_high(attended, w_o))
    middle = resident + branch
    normed2 = low(rms_scale(middle, ff_gain))
    gate = low_back(product_high(normed2, w_gate))
    upward = low_back(product_high(normed2, w_up))
    activated = low(jax.nn.silu(gate) * upward)
    return middle + product_high(activated, w_down)

def reference(hidden_in, out_grad, seq_lengths, norm_gain, w_z, w_x, w_bc, w_dt, conv_x, conv_bc, dt_bias, a_log, d_skip, w_q, key_matrix, value_matrix, w_o, w_out, ff_gain, w_gate, w_up, w_down):
    params = tuple((item.astype(jnp.float32) for item in (norm_gain, w_z, w_x, w_bc, w_dt, conv_x, conv_bc, dt_bias, a_log, d_skip, w_q, key_matrix, value_matrix, w_o, w_out, ff_gain, w_gate, w_up, w_down)))
    inputs = hidden_in.astype(jnp.float32).reshape(N_FSDP, ROWS, MODEL_WIDTH)
    cotangents = out_grad.astype(jnp.float32).reshape(N_FSDP, ROWS, MODEL_WIDTH)

    def shard(totals, item):
        resident, cotangent, lengths = item
        segment, position = doc_tables(lengths, ROWS)
        result, pull = jax.vjp(lambda value, weights: layer(value, segment, position, weights), resident, params)
        resident_grad, weight_grads = pull(cotangent)
        totals = jax.tree.map(lambda left, right: left + right, totals, weight_grads)
        return (totals, (result.astype(jnp.bfloat16), resident_grad.astype(jnp.bfloat16)))
    zeros = jax.tree.map(jnp.zeros_like, params)
    totals, (results, resident_grads) = lax.scan(shard, zeros, (inputs, cotangents, seq_lengths))
    return (results.reshape(TOKENS, MODEL_WIDTH), resident_grads.reshape(TOKENS, MODEL_WIDTH), totals[0], totals[1], totals[2], totals[3], totals[4], totals[5], totals[6], totals[7], totals[8], totals[9], totals[10], totals[11], totals[12], totals[13], totals[14], totals[15], totals[16], totals[17], totals[18])
```

```python
from functools import partial
import math

import jax
import jax.numpy as jnp
from jax import lax
from jax.sharding import PartitionSpec as P

HEAD_WIDTH = 64
NS = 128
SPAN = 256
ATT_BLOCK = 512


EPSILON = 1e-05
ROPE_BASE = 10000.0
HIGH = lax.Precision.HIGH
MASKED = -1e30


def product(left, right):
    return jnp.dot(left, right, preferred_element_type=jnp.float32)


def product_t(left, right):
    return lax.dot_general(
        left, right, (((1,), (1,)), ((), ())), preferred_element_type=jnp.float32
    )


def product_tn(left, right):
    return lax.dot_general(
        left, right, (((0,), (0,)), ((), ())), preferred_element_type=jnp.float32
    )


def doc_tables(lengths, row_count):
    ends = jnp.cumsum(lengths)
    index = jnp.arange(row_count, dtype=jnp.int32)
    segment = jnp.sum((index[:, None] >= ends[None, :]).astype(jnp.int32), axis=1)
    starts = ends - lengths
    member = segment[:, None] == jnp.arange(lengths.shape[0], dtype=jnp.int32)[None, :]
    begin = jnp.sum(jnp.where(member, starts[None, :], 0), axis=1)
    return (segment, index - begin)


def shard_sum(term):
    return lax.psum_scatter(
        term.astype(jnp.bfloat16), "fsdp", scatter_dimension=0, tiled=True
    ).astype(jnp.float32)


def rms_scale(values, gain):
    factor = lax.rsqrt(jnp.mean(values * values, axis=-1, keepdims=True) + EPSILON)
    return values * factor * gain


def swiglu(gate, upward):
    return jax.nn.silu(gate) * upward


def causal_conv(values, taps, segment):
    width = taps.shape[0]
    total = values * taps[width - 1]
    for delay in range(1, width):
        earlier = jnp.concatenate(
            [jnp.zeros((delay, values.shape[1]), values.dtype), values[:-delay]], axis=0
        )
        joined = jnp.concatenate(
            [
                jnp.zeros((delay,), values.dtype),
                (segment[delay:] == segment[:-delay]).astype(values.dtype),
            ]
        )
        total = total + earlier * joined[:, None] * taps[width - 1 - delay]
    return total


def rotate(values, position):
    row_count = values.shape[0]
    shaped = values.reshape(row_count, -1, HEAD_WIDTH)
    halfway = HEAD_WIDTH // 2
    frequency = ROPE_BASE ** (-2.0 * jnp.arange(halfway, dtype=jnp.float32) / HEAD_WIDTH)
    angle = position.astype(jnp.float32)[:, None, None] * frequency[None, None, :]
    cosine = jnp.cos(angle)
    sine = jnp.sin(angle)
    first = shaped[..., :halfway]
    second = shaped[..., halfway:]
    turned = jnp.concatenate(
        [first * cosine - second * sine, second * cosine + first * sine], axis=-1
    )
    return turned.reshape(row_count, -1)


def span_scan(x_heads, b_vectors, c_vectors, step_size, rate, segment):
    row_count, heads, head_size = x_heads.shape
    count = row_count // SPAN
    inside = jnp.arange(SPAN, dtype=jnp.int32)
    lower = inside[:, None] >= inside[None, :]

    def advance(carry, item):
        state, previous = carry
        block_x, block_b, block_c, block_step, block_seg = item
        decay_factor = jnp.cumsum(block_step * rate[None, :], axis=0)
        allowed = lower & (block_seg[:, None] == block_seg[None, :])
        spread = jnp.where(
            allowed[:, :, None], decay_factor[:, None, :] - decay_factor[None, :, :], MASKED
        )
        inner = jnp.dot(block_c, block_b.T, precision=HIGH, preferred_element_type=jnp.float32)
        mixing = jnp.exp(spread) * inner[:, :, None] * block_step[None, :, :]
        output = jnp.einsum("tsh,shp->thp", mixing, block_x, precision=HIGH)
        carried = (block_seg == previous).astype(jnp.float32)[:, None] * jnp.exp(decay_factor)
        output = (
            output + jnp.einsum("tn,hpn->thp", block_c, state, precision=HIGH) * carried[:, :, None]
        )
        tail = (
            (block_seg == block_seg[-1]).astype(jnp.float32)[:, None]
            * jnp.exp(decay_factor[-1][None, :] - decay_factor)
            * block_step
        )
        state = state * carried[-1][:, None, None] + jnp.einsum(
            "sh,shp,sn->hpn", tail, block_x, block_b, precision=HIGH
        )
        return ((state, block_seg[-1]), output)

    items = (
        x_heads.reshape(count, SPAN, heads, head_size),
        b_vectors.reshape(count, SPAN, -1),
        c_vectors.reshape(count, SPAN, -1),
        step_size.reshape(count, SPAN, heads),
        segment.reshape(count, SPAN),
    )
    start = (
        jnp.zeros((heads, head_size, b_vectors.shape[1]), jnp.float32),
        jnp.asarray(-1, jnp.int32),
    )
    _, outputs = lax.scan(jax.checkpoint(advance), start, items)
    return outputs.reshape(row_count, heads, head_size)


def mixer_middle(
    z_branch, x_branch, pair_branch, step_raw, conv_own, conv_pair, bias, log_rate, skip, segment
):
    row_count = z_branch.shape[0]
    x_active = jax.nn.silu(causal_conv(x_branch, conv_own, segment))
    pair_active = jax.nn.silu(causal_conv(pair_branch, conv_pair, segment))
    step_size = jax.nn.softplus(step_raw + bias[None, :])
    rate = -jnp.exp(log_rate)
    heads = bias.shape[0]
    x_heads = x_active.reshape(row_count, heads, HEAD_WIDTH)
    states = span_scan(x_heads, pair_active[:, :NS], pair_active[:, NS:], step_size, rate, segment)
    result = states + skip[None, :, None] * x_heads
    return result.reshape(row_count, heads * HEAD_WIDTH) * jax.nn.silu(z_branch)


def attend_forward(query, keys, values, segment):
    row_count = query.shape[0]
    kv_heads = keys.shape[1] // HEAD_WIDTH
    group = query.shape[1] // keys.shape[1]
    key_heads = keys.reshape(row_count, kv_heads, HEAD_WIDTH)
    value_heads = values.reshape(row_count, kv_heads, HEAD_WIDTH)
    index = jnp.arange(row_count, dtype=jnp.int32)
    count = row_count // ATT_BLOCK
    scale = 1.0 / math.sqrt(HEAD_WIDTH)

    def block(item):
        query_block, seg_block, row_block = item
        score = (
            jnp.einsum("qkgd,skd->kgqs", query_block, key_heads, preferred_element_type=jnp.float32)
            * scale
        )
        allowed = (seg_block[:, None] == segment[None, :]) & (row_block[:, None] >= index[None, :])
        score = jnp.where(allowed[None, None], score, MASKED)
        peak = jnp.max(score, axis=-1, keepdims=True)
        weight = jnp.exp(score - peak)
        total = jnp.sum(weight, axis=-1, keepdims=True)
        prob = (weight / total).astype(jnp.bfloat16)
        output = jnp.einsum("kgqs,skd->qkgd", prob, value_heads, preferred_element_type=jnp.float32)
        return (
            output.reshape(ATT_BLOCK, kv_heads * group * HEAD_WIDTH),
            (peak + jnp.log(total))[..., 0],
        )

    blocks = (
        query.reshape(count, ATT_BLOCK, kv_heads, group, HEAD_WIDTH),
        segment.reshape(count, ATT_BLOCK),
        index.reshape(count, ATT_BLOCK),
    )
    outputs, logsum = lax.map(block, blocks)
    return (outputs.reshape(row_count, -1), logsum)


def attend_backward(query, keys, values, segment, logsum, attended_grad):
    row_count = query.shape[0]
    kv_heads = keys.shape[1] // HEAD_WIDTH
    group = query.shape[1] // keys.shape[1]
    key_heads = keys.reshape(row_count, kv_heads, HEAD_WIDTH)
    value_heads = values.reshape(row_count, kv_heads, HEAD_WIDTH)
    index = jnp.arange(row_count, dtype=jnp.int32)
    count = row_count // ATT_BLOCK
    scale = 1.0 / math.sqrt(HEAD_WIDTH)

    def block(carry, item):
        key_total, value_total = carry
        query_block, seg_block, row_block, logsum_block, grad_block = item
        score = (
            jnp.einsum("qkgd,skd->kgqs", query_block, key_heads, preferred_element_type=jnp.float32)
            * scale
        )
        allowed = (seg_block[:, None] == segment[None, :]) & (row_block[:, None] >= index[None, :])
        score = jnp.where(allowed[None, None], score, MASKED)
        prob = jnp.exp(score - logsum_block[..., None])
        prob_low = prob.astype(jnp.bfloat16)
        prob_grad = jnp.einsum(
            "qkgd,skd->kgqs", grad_block, value_heads, preferred_element_type=jnp.float32
        )
        centre = jnp.sum(prob * prob_grad, axis=-1, keepdims=True)
        score_grad = (prob * (prob_grad - centre)).astype(jnp.bfloat16)
        query_grad = (
            jnp.einsum("kgqs,skd->qkgd", score_grad, key_heads, preferred_element_type=jnp.float32)
            * scale
        )
        key_total = (
            key_total
            + jnp.einsum(
                "kgqs,qkgd->skd", score_grad, query_block, preferred_element_type=jnp.float32
            )
            * scale
        )
        value_total = value_total + jnp.einsum(
            "kgqs,qkgd->skd", prob_low, grad_block, preferred_element_type=jnp.float32
        )
        return ((key_total, value_total), query_grad.reshape(ATT_BLOCK, -1))

    blocks = (
        query.reshape(count, ATT_BLOCK, kv_heads, group, HEAD_WIDTH),
        segment.reshape(count, ATT_BLOCK),
        index.reshape(count, ATT_BLOCK),
        logsum,
        attended_grad.reshape(count, ATT_BLOCK, kv_heads, group, HEAD_WIDTH),
    )
    empty = jnp.zeros((row_count, kv_heads, HEAD_WIDTH), jnp.float32)
    (key_total, value_total), query_grads = lax.scan(block, (empty, empty), blocks)
    return (
        query_grads.reshape(row_count, -1),
        key_total.reshape(row_count, -1),
        value_total.reshape(row_count, -1),
    )


def shards(
    hidden_in,
    out_grad,
    seq_lengths,
    norm_gain,
    w_z,
    w_x,
    w_bc,
    w_dt,
    conv_x,
    conv_bc,
    dt_bias,
    a_log,
    d_skip,
    w_q,
    key_matrix,
    value_matrix,
    w_o,
    w_out,
    ff_gain,
    w_gate,
    w_up,
    w_down,
):
    pieces = lax.axis_size("tp")
    place = lax.axis_index("tp")
    resident = hidden_in.astype(jnp.float32)
    own_rows = resident.shape[0]
    row_count = own_rows * pieces
    segment, position = doc_tables(seq_lengths[0], row_count)
    width_here = w_x.shape[1]
    heads_here = w_dt.shape[1]
    conv_here = lax.dynamic_slice_in_dim(conv_x, place * width_here, width_here, 1)
    bias_here = lax.dynamic_slice_in_dim(dt_bias, place * heads_here, heads_here, 0)
    rate_here = lax.dynamic_slice_in_dim(a_log, place * heads_here, heads_here, 0)
    skip_here = lax.dynamic_slice_in_dim(d_skip, place * heads_here, heads_here, 0)
    full_z, full_x, full_bc, full_dt, full_q, full_k, full_v, full_o, full_out = (
        lax.all_gather(w_z, "fsdp", axis=0, tiled=True),
        lax.all_gather(w_x, "fsdp", axis=0, tiled=True),
        lax.all_gather(w_bc, "fsdp", axis=0, tiled=True),
        lax.all_gather(w_dt, "fsdp", axis=0, tiled=True),
        lax.all_gather(w_q, "fsdp", axis=0, tiled=True),
        lax.all_gather(key_matrix, "fsdp", axis=0, tiled=True),
        lax.all_gather(value_matrix, "fsdp", axis=0, tiled=True),
        lax.all_gather(w_o.T, "fsdp", axis=0, tiled=True).T,
        lax.all_gather(w_out.T, "fsdp", axis=0, tiled=True).T,
    )
    normed_own, norm_pull = jax.vjp(rms_scale, resident, norm_gain)
    normed = lax.all_gather(normed_own.astype(jnp.bfloat16), "tp", axis=0, tiled=True)
    z_branch = product(normed, full_z)
    x_branch = product(normed, full_x)
    pair_branch = product(normed, full_bc)
    step_raw = product(normed, full_dt)
    gated, mixer_pull = jax.vjp(
        partial(mixer_middle, segment=segment),
        z_branch,
        x_branch,
        pair_branch,
        step_raw,
        conv_here,
        conv_bc,
        bias_here,
        rate_here,
        skip_here,
    )
    gated_low = gated.astype(jnp.bfloat16)
    query_rot, query_pull = jax.vjp(partial(rotate, position=position), product(normed, full_q))
    key_rot, key_pull = jax.vjp(partial(rotate, position=position), product(normed, full_k))
    query = query_rot.astype(jnp.bfloat16)
    keys = key_rot.astype(jnp.bfloat16)
    values = product(normed, full_v).astype(jnp.bfloat16)
    attended, logsum = attend_forward(query, keys, values, segment)
    attended_low = attended.astype(jnp.bfloat16)
    branch_terms = product(gated_low, full_out) + product(attended_low, full_o)
    branch_own = lax.psum_scatter(branch_terms, "tp", scatter_dimension=0, tiled=True)
    middle = resident + branch_own
    normed2_own, norm2_pull = jax.vjp(rms_scale, middle, ff_gain)
    normed2 = lax.all_gather(normed2_own.astype(jnp.bfloat16), "tp", axis=0, tiled=True)
    full_gate, full_up, full_down = (
        lax.all_gather(w_gate, "fsdp", axis=0, tiled=True),
        lax.all_gather(w_up, "fsdp", axis=0, tiled=True),
        lax.all_gather(w_down.T, "fsdp", axis=0, tiled=True).T,
    )
    gate = product(normed2, full_gate)
    upward = product(normed2, full_up)
    activated, swiglu_pull = jax.vjp(swiglu, gate, upward)
    activated_low = activated.astype(jnp.bfloat16)
    feedforward_local = lax.psum_scatter(
        product(activated_low, full_down).astype(jnp.bfloat16),
        "tp",
        scatter_dimension=0,
        tiled=True,
    ).astype(jnp.float32)
    layer_out = (middle + feedforward_local).astype(jnp.bfloat16)
    cotangent_full = lax.all_gather(out_grad, "tp", axis=0, tiled=True)
    gate_grad, up_grad = swiglu_pull(product_t(cotangent_full, full_down))
    gate_low = gate_grad.astype(jnp.bfloat16)
    up_low = up_grad.astype(jnp.bfloat16)
    normed2_terms = product_t(gate_low, full_gate) + product_t(up_low, full_up)
    gate_term = product_tn(normed2, gate_low)
    up_term = product_tn(normed2, up_low)
    down_term = product_tn(cotangent_full, activated_low)
    gate_wgrad, up_wgrad, down_wgrad = (
        shard_sum(gate_term),
        shard_sum(up_term),
        shard_sum(down_term).T,
    )
    normed2_grad = lax.psum_scatter(
        normed2_terms.astype(jnp.bfloat16), "tp", scatter_dimension=0, tiled=True
    ).astype(jnp.float32)
    middle_from_norm, ff_gain_grad = norm2_pull(normed2_grad)
    middle_grad = out_grad.astype(jnp.float32) + middle_from_norm
    branch_full = lax.all_gather(middle_grad.astype(jnp.bfloat16), "tp", axis=0, tiled=True)
    out_term = product_tn(branch_full, gated_low)
    o_term = product_tn(branch_full, attended_low)
    attended_grad = product_t(branch_full, full_o).astype(jnp.bfloat16)
    gated_grad = product_t(branch_full, full_out)
    (
        z_grad,
        x_grad,
        pair_grad,
        step_grad,
        conv_grad,
        conv_pair_grad,
        bias_grad,
        rate_grad,
        skip_grad,
    ) = mixer_pull(gated_grad)
    query_grad_rot, key_grad_rot, value_grad = attend_backward(
        query, keys, values, segment, logsum, attended_grad
    )
    (query_grad,) = query_pull(query_grad_rot)
    (key_grad,) = key_pull(key_grad_rot)
    z_low = z_grad.astype(jnp.bfloat16)
    x_low = x_grad.astype(jnp.bfloat16)
    step_low = step_grad.astype(jnp.bfloat16)
    query_low = query_grad.astype(jnp.bfloat16)
    key_low = key_grad.astype(jnp.bfloat16)
    value_low = value_grad.astype(jnp.bfloat16)
    normed_terms = (
        product_t(z_low, full_z)
        + product_t(x_low, full_x)
        + product_t(step_low, full_dt)
        + product_t(query_low, full_q)
        + product_t(key_low, full_k)
        + product_t(value_low, full_v)
        + jnp.dot(
            pair_grad,
            full_bc.astype(jnp.float32).T,
            precision=HIGH,
            preferred_element_type=jnp.float32,
        )
    )
    normed_grad = lax.psum_scatter(
        normed_terms.astype(jnp.bfloat16), "tp", scatter_dimension=0, tiled=True
    ).astype(jnp.float32)
    resident_from_norm, gain_grad = norm_pull(normed_grad)
    input_grad = (middle_grad + resident_from_norm).astype(jnp.bfloat16)
    z_term = product_tn(normed, z_low)
    x_term = product_tn(normed, x_low)
    step_term = product_tn(normed, step_low)
    query_term = product_tn(normed, query_low)
    key_term = product_tn(normed, key_low)
    value_term = product_tn(normed, value_low)
    pair_wgrad = jnp.matmul(normed.T, pair_grad, precision=HIGH)
    (
        z_wgrad,
        x_wgrad,
        step_wgrad,
        query_wgrad,
        key_wgrad,
        value_weight_gradient,
        o_wgrad,
        out_wgrad,
    ) = (
        shard_sum(z_term),
        shard_sum(x_term),
        shard_sum(step_term),
        shard_sum(query_term),
        shard_sum(key_term),
        shard_sum(value_term),
        shard_sum(o_term).T,
        shard_sum(out_term).T,
    )
    conv_full = lax.dynamic_update_slice_in_dim(
        jnp.zeros(conv_x.shape, jnp.float32), conv_grad, place * width_here, 1
    )
    bias_full = lax.dynamic_update_slice_in_dim(
        jnp.zeros(dt_bias.shape, jnp.float32), bias_grad, place * heads_here, 0
    )
    rate_full = lax.dynamic_update_slice_in_dim(
        jnp.zeros(a_log.shape, jnp.float32), rate_grad, place * heads_here, 0
    )
    skip_full = lax.dynamic_update_slice_in_dim(
        jnp.zeros(d_skip.shape, jnp.float32), skip_grad, place * heads_here, 0
    )
    (
        gain_total,
        conv_total,
        conv_pair_total,
        bias_total,
        rate_total,
        skip_total,
        ff_gain_total,
    ) = lax.psum(
        (
            gain_grad,
            conv_full,
            conv_pair_grad,
            bias_full,
            rate_full,
            skip_full,
            ff_gain_grad,
        ),
        ("fsdp", "tp"),
    )
    pair_shard = lax.psum(shard_sum(pair_wgrad), "tp")
    return (
        layer_out,
        input_grad,
        gain_total,
        z_wgrad,
        x_wgrad,
        pair_shard,
        step_wgrad,
        conv_total,
        conv_pair_total,
        bias_total,
        rate_total,
        skip_total,
        query_wgrad,
        key_wgrad,
        value_weight_gradient,
        o_wgrad,
        out_wgrad,
        ff_gain_total,
        gate_wgrad,
        up_wgrad,
        down_wgrad,
    )


def solution(mesh):
    in_specs = (
        P(("fsdp", "tp"), None),
        P(("fsdp", "tp"), None),
        P("fsdp", None),
        P(),
        P("fsdp", "tp"),
        P("fsdp", "tp"),
        P("fsdp", None),
        P("fsdp", "tp"),
        P(),
        P(),
        P(),
        P(),
        P(),
        P("fsdp", "tp"),
        P("fsdp", "tp"),
        P("fsdp", "tp"),
        P("tp", "fsdp"),
        P("tp", "fsdp"),
        P(),
        P("fsdp", "tp"),
        P("fsdp", "tp"),
        P("tp", "fsdp"),
    )
    out_specs = (
        P(("fsdp", "tp"), None),
        P(("fsdp", "tp"), None),
        P(),
        P("fsdp", "tp"),
        P("fsdp", "tp"),
        P("fsdp", None),
        P("fsdp", "tp"),
        P(),
        P(),
        P(),
        P(),
        P(),
        P("fsdp", "tp"),
        P("fsdp", "tp"),
        P("fsdp", "tp"),
        P("tp", "fsdp"),
        P("tp", "fsdp"),
        P(),
        P("fsdp", "tp"),
        P("fsdp", "tp"),
        P("tp", "fsdp"),
    )
    return jax.shard_map(shards, mesh=mesh, in_specs=in_specs, out_specs=out_specs, check_vma=False)
```
